32 devices in a mesh: row: 4 (over y, x), col: 8 (over z, core).
Axes of the slice: x: 2, y: 2, z: 4, core: 2. Of those that a mesh axis runs over, the one named last changes fastest.
Arguments:
- z_slab: float32 [1024, 1024], P('col', 'row'), may hold values from -6 to 6
- prev_factor: bfloat16 [1024, 32768], P('row', 'col'), may hold values from -0.03125 to 0.03125
- prev_solution: bfloat16 [1024, 32768], P(None, 'col'), may hold values from -6 to 6
- slab_factor: bfloat16 [1024, 1024], P('row'), may hold values from -0.09375 to 0.09375
- diag_inverse: bfloat16 [1024, 256], P('row'), may hold values from -1 to 2, as said below
Outputs:
- solved: float32 [1024, 1024], P('col', 'row')
The draws below stay inside these ranges and needn't reach their ends.
Inputs may be any that keep to these rules, and one draw needn't show every extreme that they name: `diag_inverse`: each 256 x 256 block is lower triangular with its diagonal between 1 and 2.
All inputs are finite; a program needn't handle non-finite values.
Results may differ from the reference program's by a relative error of at most 0.0003.
Values sent between devices are 32-bit elements; how exact they have to be, the bound alone decides.
A program may use at most 64 MiB of HBM per device.

```python
import math
import jax
import jax.numpy as jnp
from jax import lax

BLOCK = 256
SAMPLES = 1024
SLAB = 1024
PREV = 32768
N_ROW = 4


def draw_diag_inverse(key, part):
    first_key, second_key = jax.random.split(key)
    noise = jnp.clip(jax.random.normal(first_key, (SLAB, BLOCK), jnp.float32), -3.0, 3.0)
    diagonal = jax.random.uniform(second_key, (SLAB, BLOCK), jnp.float32, 1.0, 2.0)
    inner = jnp.arange(SLAB)[:, None] % BLOCK
    column = jnp.arange(BLOCK)[None, :]
    lower = noise * (0.5 / math.sqrt(BLOCK))
    values = jnp.where(column == inner, diagonal, jnp.where(column < inner, lower, 0.0))
    return values.astype(jnp.bfloat16)


def spiked(drawn, own_key, source, target, shards_of, factor):
    def block_of(axis_at):
        return (jnp.arange(drawn.shape[axis_at]) // (drawn.shape[axis_at] // shards_of)).reshape((-1,) + (1,) * (drawn.ndim - 1 - axis_at))

    first = jax.random.permutation(own_key, shards_of)[block_of(target)]
    far = (block_of(target) + shards_of // 2) % shards_of
    return jnp.where((block_of(source) == first) | (block_of(source) == far), factor * drawn, drawn)


def block_levels(own_key, dims, shards, smallest, top_value):
    def one(position, blocks):
        heights = jax.random.uniform(jax.random.fold_in(jax.random.fold_in(own_key, 6), position), (blocks,), jnp.float32, smallest / len(shards), top_value / len(shards))
        return jnp.repeat(jnp.exp(heights), dims[position] // blocks).reshape((-1,) + (1,) * (len(dims) - position - 1))

    level = one(*shards[0])
    for cut in shards[1:]:
        level = level * one(*cut)
    return level


def scatter_about(key, dims, width, most, cuts=(), dtype=jnp.bfloat16):
    drawn = width * jax.random.normal(key, dims, jnp.float32)
    if cuts:
        drawn = drawn * block_levels(key, dims, cuts, -0.22, 0.18)
    return jnp.clip(drawn, -most, most).astype(dtype)


def bell_draw_with(key, shape, width, bound, shards, heavy, kind=jnp.bfloat16):
    values = width * jax.random.normal(key, shape, jnp.float32)
    if shards:
        values = values * block_levels(key, shape, shards, -0.22, 0.18)
    return jnp.clip(spiked(values, jax.random.fold_in(key, 3), *heavy), -bound, bound).astype(kind)


def setup_inputs(seed: int = 0) -> dict:
    key_list = jax.random.split(jax.random.key(seed), 6)
    return {
        "z_slab": scatter_about(key_list[0], (SAMPLES, SLAB), 1.0, 6.0, ((0, 8), (1, 4)), jnp.float32),
        "prev_factor": scatter_about(key_list[1], (SLAB, PREV), PREV ** -0.5, 0.03125, ((0, 4), (1, 8))),
        "prev_solution": bell_draw_with(key_list[2], (SAMPLES, PREV), 1.0, 6.0, ((1, 8),), (1, 0, 8, 2.0)),
        "slab_factor": scatter_about(key_list[3], (SLAB, SLAB), (4 * SLAB) ** -0.5, 0.09375, ((0, 4),)),
        "diag_inverse": draw_diag_inverse(jax.random.fold_in(key_list[5], 71), 0),
    }


def precise_dot(left, right):
    return lax.dot_general(left, right, (((1,), (1,)), ((), ())), precision=lax.Precision.HIGHEST, preferred_element_type=jnp.float32)


def reference(z_slab, prev_factor, prev_solution, slab_factor, diag_inverse):
    fan_sum = lax.dot_general(prev_solution, prev_factor, (((1,), (1,)), ((), ())), preferred_element_type=jnp.float32)
    remainder = z_slab - fan_sum
    factor = slab_factor.astype(jnp.float32)
    inverse = diag_inverse.astype(jnp.float32)
    pieces = []
    for block_index in range(N_ROW):
        lower = block_index * BLOCK
        updates = jnp.zeros((z_slab.shape[0], BLOCK), jnp.float32)
        for earlier in range(block_index):
            updates = updates + precise_dot(pieces[earlier], factor[lower:lower + BLOCK, earlier * BLOCK:(earlier + 1) * BLOCK])
        current = remainder[:, lower:lower + BLOCK] - updates
        pieces.append(precise_dot(current, inverse[lower:lower + BLOCK, :]))
    return jnp.concatenate(pieces, axis=1)
```

```python
import functools

import jax
import jax.numpy as jnp
from jax import lax
from jax.experimental import pallas as pl
from jax.experimental.pallas import tpu as pltpu
from jax.sharding import PartitionSpec as P

MESH = pl.DeviceIdType.MESH
CORES = 2
HALVES = 2


def dot_t(left, right):
    return lax.dot_general(
        left, right, (((1,), (1,)), ((), ())), preferred_element_type=jnp.float32
    )


def dot_split(left, right):
    high = left.astype(jnp.bfloat16)
    low = (left - high.astype(jnp.float32)).astype(jnp.bfloat16)
    return dot_t(high, right) + dot_t(low, right)


def kernel(
    n_row, n_col,
    z_hbm, pf_hbm, ps_hbm, sf_hbm, di_hbm,
    out_ref,
    z_v, pf, ps, sf, di, part, give, got, line, sol,
    load_sem, ps_sem, core_send, core_recv, line_send, line_recv, sol_send, sol_recv,
):
    n_z = n_col // CORES
    m, block = z_v.shape
    mh = m // HALVES
    row = lax.axis_index("row")
    col = lax.axis_index("col")
    p = col // CORES
    core = lax.rem(col, CORES)
    mate = col + 1 - 2 * core
    chunk = CORES * m
    low_half = p < n_z // 2

    barrier = pltpu.get_barrier_semaphore()

    def greet(device):
        pl.semaphore_signal(barrier, inc=1, device_id=device, device_id_type=MESH)

    greet({"col": mate})

    @pl.when(p > 0)
    def _():
        greet({"col": col - CORES})

    @pl.when(p < n_z - 1)
    def _():
        greet({"col": col + CORES})

    for other in range(n_row):
        @pl.when(row != other)
        def _():
            greet({"row": other})

    def target(i):
        return jnp.where(low_half, n_z - 1 - i, i)

    def ps_copy(i):
        rows = pl.ds(pl.multiple_of(target(i) * chunk, chunk), chunk)
        return pltpu.make_async_copy(ps_hbm.at[rows], ps.at[rows], ps_sem.at[i])

    pf_copy = pltpu.make_async_copy(pf_hbm, pf, load_sem.at[0])
    z_copy = pltpu.make_async_copy(z_hbm, z_v, load_sem.at[1])
    sf_copy = pltpu.make_async_copy(sf_hbm, sf, load_sem.at[2])
    di_copy = pltpu.make_async_copy(di_hbm, di, load_sem.at[3])
    pf_copy.start()
    for i in range(n_z):
        ps_copy(i).start()
    z_copy.start()
    sf_copy.start()
    di_copy.start()
    pf_copy.wait()

    def multiply(i):
        t = target(i)
        ps_copy(i).wait()
        rows = pl.multiple_of(t * chunk, chunk)
        theirs = ps[pl.ds(pl.multiple_of(rows + (1 - core) * m, m), m), :]
        give[t] = dot_t(theirs, pf[...])
        mine = ps[pl.ds(pl.multiple_of(rows + core * m, m), m), :]
        part[t] = dot_t(mine, pf[...])

    def core_copy(t):
        return pltpu.make_async_remote_copy(
            src_ref=give.at[t], dst_ref=got.at[t],
            send_sem=core_send.at[t], recv_sem=core_recv.at[t],
            device_id={"col": mate}, device_id_type=MESH,
        )

    def half(h):
        return pl.ds(h * mh, mh)

    def line_move(source, d, t, h):
        return pltpu.make_async_remote_copy(
            src_ref=source, dst_ref=line.at[d, t, half(h)],
            send_sem=line_send.at[d, t, h], recv_sem=line_recv.at[d, t, h],
            device_id={"col": col + CORES * (1 - 2 * d)}, device_id_type=MESH,
        )

    def pair_sum(i):
        t = target(i)
        core_copy(t).wait_recv()
        part[t] = part[t] + got[t]

        @pl.when((p == 0) & (t > 0))
        def _():
            for h in range(HALVES):
                line_move(part.at[t, half(h)], 0, t, h).start()

        @pl.when((p == n_z - 1) & (t < n_z - 1))
        def _():
            for h in range(HALVES):
                line_move(part.at[t, half(h)], 1, t, h).start()

    multiply(0)
    pl.semaphore_wait(
        barrier,
        n_row + (p > 0).astype(jnp.int32) + (p < n_z - 1).astype(jnp.int32),
    )
    core_copy(target(0)).start()

    @pl.loop(1, n_z)
    def _(i):
        multiply(i)
        core_copy(target(i)).start()
        pair_sum(i - 1)

    pair_sum(n_z - 1)

    first = jnp.where(low_half, 0, 1)
    inner = (p > 0) & (p < n_z - 1)

    @pl.loop(0, n_z - 1)
    def _(i):
        for e in range(2):
            d = first if e == 0 else 1 - first
            t = jnp.where(d == 0, n_z - 1 - i, i)

            @pl.when(inner & jnp.where(d == 0, t > p, t < p))
            def _():
                for h in range(HALVES):
                    line_move(line.at[d, t, half(h)], d, t, h).wait_recv()
                    line[d, t, half(h)] = line[d, t, half(h)] + part[t, half(h)]
                    line_move(line.at[d, t, half(h)], d, t, h).start()

    z_copy.wait()
    sf_copy.wait()
    di_copy.wait()

    def sol_copy(owner, h, to):
        return pltpu.make_async_remote_copy(
            src_ref=out_ref.at[half(h)], dst_ref=sol.at[owner, half(h)],
            send_sem=sol_send.at[to, h], recv_sem=sol_recv.at[owner, h],
            device_id={"row": to}, device_id_type=MESH,
        )

    for h in range(HALVES):
        part[p, half(h)] = z_v[half(h)] - part[p, half(h)]

        @pl.when(p > 0)
        def _():
            line_move(line.at[0, p, half(h)], 0, p, h).wait_recv()
            part[p, half(h)] = part[p, half(h)] - line[0, p, half(h)]

        @pl.when(p < n_z - 1)
        def _():
            line_move(line.at[1, p, half(h)], 1, p, h).wait_recv()
            part[p, half(h)] = part[p, half(h)] - line[1, p, half(h)]

        @pl.loop(0, row)
        def _(j):
            sol_copy(j, h, row).wait_recv()
            columns = pl.ds(pl.multiple_of(j * block, block), block)
            part[p, half(h)] = part[p, half(h)] - dot_split(sol[j, half(h)], sf[:, columns])

        out_ref[half(h)] = dot_split(part[p, half(h)], di[...])

        @pl.loop(row + 1, n_row)
        def _(j):
            sol_copy(row, h, j).start()

    for h in range(HALVES):
        @pl.loop(row + 1, n_row)
        def _(j):
            sol_copy(row, h, j).wait_send()

    @pl.loop(0, n_z)
    def _(t):
        core_copy(t).wait_send()
        for h in range(HALVES):
            @pl.when((p < n_z - 1) & (t > p))
            def _():
                line_move(line.at[0, t, half(h)], 0, t, h).wait_send()

            @pl.when((p > 0) & (t < p))
            def _():
                line_move(line.at[1, t, half(h)], 1, t, h).wait_send()


def on_device(n_row, n_col, z_slab, prev_factor, prev_solution, slab_factor, diag_inverse):
    m, block = z_slab.shape
    n_z = n_col // CORES
    anywhere = pl.BlockSpec(memory_space=pl.ANY)
    f32 = jnp.float32
    return pl.pallas_call(
        functools.partial(kernel, n_row, n_col),
        out_shape=jax.ShapeDtypeStruct((m, block), f32),
        in_specs=[anywhere] * 5,
        out_specs=pl.BlockSpec(memory_space=pltpu.VMEM),
        scratch_shapes=[
            pltpu.VMEM(z_slab.shape, f32),
            pltpu.VMEM(prev_factor.shape, prev_factor.dtype),
            pltpu.VMEM(prev_solution.shape, prev_solution.dtype),
            pltpu.VMEM(slab_factor.shape, slab_factor.dtype),
            pltpu.VMEM(diag_inverse.shape, diag_inverse.dtype),
            pltpu.VMEM((n_z, m, block), f32),
            pltpu.VMEM((n_z, m, block), f32),
            pltpu.VMEM((n_z, m, block), f32),
            pltpu.VMEM((2, n_z, m, block), f32),
            pltpu.VMEM((n_row, m, block), f32),
            pltpu.SemaphoreType.DMA((4,)),
            pltpu.SemaphoreType.DMA((n_z,)),
            pltpu.SemaphoreType.DMA((n_z,)),
            pltpu.SemaphoreType.DMA((n_z,)),
            pltpu.SemaphoreType.DMA((2, n_z, HALVES)),
            pltpu.SemaphoreType.DMA((2, n_z, HALVES)),
            pltpu.SemaphoreType.DMA((n_row, HALVES)),
            pltpu.SemaphoreType.DMA((n_row, HALVES)),
        ],
        compiler_params=pltpu.CompilerParams(
            collective_id=0, has_side_effects=True, vmem_limit_bytes=40 * 2**20
        ),
    )(z_slab, prev_factor, prev_solution, slab_factor, diag_inverse)


def solution(mesh):
    in_specs = (P("col", "row"), P("row", "col"), P(None, "col"), P("row", None), P("row", None))
    return jax.shard_map(
        functools.partial(on_device, mesh.shape["row"], mesh.shape["col"]),
        mesh=mesh, in_specs=in_specs, out_specs=P("col", "row"), check_vma=False,
    )
```

```python
import functools

import jax
import jax.numpy as jnp
from jax import lax
from jax.experimental import pallas as pl
from jax.experimental.pallas import tpu as pltpu
from jax.sharding import PartitionSpec as P

MESH = pl.DeviceIdType.MESH
CORES = 2
HALVES = 4
GATHER_ROWS = 4


def dot_t(left, right):
    return lax.dot_general(
        left, right, (((1,), (1,)), ((), ())), preferred_element_type=jnp.float32
    )


def dot_split(left, right):
    high = left.astype(jnp.bfloat16)
    low = (left - high.astype(jnp.float32)).astype(jnp.bfloat16)
    return dot_t(high, right) + dot_t(low, right)


def dot_n(left, right):
    return jnp.dot(left, right, preferred_element_type=jnp.float32)


def split(value):
    high = value.astype(jnp.bfloat16)
    return high, (value - high.astype(jnp.float32)).astype(jnp.bfloat16)


def kernel(
    n_row, n_col,
    z_hbm, pf_hbm, ps_hbm, sf_hbm, di_hbm,
    out_ref,
    z_v, pf, ps, sf, di, part, give, got, line, sol,
    load_sem, ps_sem, core_send, core_recv, line_send, line_recv, sol_send, sol_recv,
    raw, coef, g_high, g_low, raw_send, raw_recv, pair_send, pair_recv,
):
    gathered = n_row <= GATHER_ROWS
    n_z = n_col // CORES
    m, block = z_v.shape
    mh = m // HALVES
    row = lax.axis_index("row")
    col = lax.axis_index("col")
    p = col // CORES
    core = lax.rem(col, CORES)
    mate = col + 1 - 2 * core
    chunk = CORES * m
    low_half = p < n_z // 2

    barrier = pltpu.get_barrier_semaphore()

    def greet(device):
        pl.semaphore_signal(barrier, inc=1, device_id=device, device_id_type=MESH)

    greet({"col": mate})

    @pl.when(p > 0)
    def _():
        greet({"col": col - CORES})

    @pl.when(p < n_z - 1)
    def _():
        greet({"col": col + CORES})

    for other in range(n_row):
        @pl.when(row != other)
        def _():
            greet({"row": other})

    def target(i):
        return jnp.where(low_half, n_z - 1 - i, i)

    def ps_copy(i):
        rows = pl.ds(pl.multiple_of(target(i) * chunk, chunk), chunk)
        return pltpu.make_async_copy(ps_hbm.at[rows], ps.at[rows], ps_sem.at[i])

    pf_copy = pltpu.make_async_copy(pf_hbm, pf, load_sem.at[0])
    z_copy = pltpu.make_async_copy(z_hbm, z_v, load_sem.at[1])
    sf_copy = pltpu.make_async_copy(sf_hbm, sf, load_sem.at[2])
    di_copy = pltpu.make_async_copy(di_hbm, di, load_sem.at[3])
    sf_copy.start()
    di_copy.start()
    pf_copy.start()
    for i in range(n_z):
        ps_copy(i).start()
    z_copy.start()

    b_half = block // 2
    own_half = pl.ds(pl.multiple_of(core * b_half, b_half), b_half)

    def raw_copy(i, j, to):
        return pltpu.make_async_remote_copy(
            src_ref=raw.at[i, j, own_half], dst_ref=raw.at[i, j, own_half],
            send_sem=raw_send.at[to, j], recv_sem=raw_recv.at[i, j],
            device_id={"row": to}, device_id_type=MESH,
        )

    def pair_copy(i, j):
        return pltpu.make_async_remote_copy(
            src_ref=raw.at[i, j, own_half], dst_ref=raw.at[i, j, own_half],
            send_sem=pair_send.at[i, j], recv_sem=pair_recv.at[i, j],
            device_id={"col": mate}, device_id_type=MESH,
        )

    def columns_of(j):
        return pl.ds(pl.multiple_of(j * block, block), block)

    sf_copy.wait()
    di_copy.wait()
    if gathered:
        @pl.when(row < n_row - 1)
        def _():
            raw[row, row, own_half] = di[own_half].astype(jnp.float32)

            @pl.loop(0, row)
            def _(j):
                raw[row, j, own_half] = sf[own_half, columns_of(j)].astype(jnp.float32)

    pf_copy.wait()

    def core_copy(t):
        return pltpu.make_async_remote_copy(
            src_ref=give.at[t], dst_ref=got.at[t],
            send_sem=core_send.at[t], recv_sem=core_recv.at[t],
            device_id={"col": mate}, device_id_type=MESH,
        )

    def multiply(i):
        t = target(i)
        ps_copy(i).wait()
        rows = pl.multiple_of(t * chunk, chunk)
        theirs = ps[pl.ds(pl.multiple_of(rows + (1 - core) * m, m), m), :]
        give[t] = dot_t(theirs, pf[...])
        if isinstance(i, int):
            pl.semaphore_wait(
                barrier,
                n_row + (p > 0).astype(jnp.int32) + (p < n_z - 1).astype(jnp.int32),
            )
        core_copy(t).start()
        mine = ps[pl.ds(pl.multiple_of(rows + core * m, m), m), :]
        part[t] = dot_t(mine, pf[...])

    def half(h):
        return pl.ds(h * mh, mh)

    def line_move(source, d, t, h):
        return pltpu.make_async_remote_copy(
            src_ref=source, dst_ref=line.at[d, t, half(h)],
            send_sem=line_send.at[d, t, h], recv_sem=line_recv.at[d, t, h],
            device_id={"col": col + CORES * (1 - 2 * d)}, device_id_type=MESH,
        )

    def pair_sum(i):
        t = target(i)
        core_copy(t).wait_recv()
        part[t] = part[t] + got[t]

        @pl.when((p == 0) & (t > 0))
        def _():
            for h in range(HALVES):
                line_move(part.at[t, half(h)], 0, t, h).start()

        @pl.when((p == n_z - 1) & (t < n_z - 1))
        def _():
            for h in range(HALVES):
                line_move(part.at[t, half(h)], 1, t, h).start()

    multiply(0)
    if gathered:
        @pl.loop(row + 1, n_row)
        def _(to):
            @pl.loop(0, row + 1)
            def _(j):
                raw_copy(row, j, to).start()

    @pl.loop(1, n_z)
    def _(i):
        multiply(i)
        pair_sum(i - 1)

    pair_sum(n_z - 1)

    first = jnp.where(low_half, 0, 1)
    inner = (p > 0) & (p < n_z - 1)

    @pl.loop(0, n_z - 1)
    def _(i):
        for e in range(2):
            d = first if e == 0 else 1 - first
            t = jnp.where(d == 0, n_z - 1 - i, i)

            @pl.when(inner & jnp.where(d == 0, t > p, t < p))
            def _():
                for h in range(HALVES):
                    line_move(line.at[d, t, half(h)], d, t, h).wait_recv()
                    line[d, t, half(h)] = line[d, t, half(h)] + part[t, half(h)]
                    line_move(line.at[d, t, half(h)], d, t, h).start()

    z_copy.wait()
    if gathered:
        @pl.loop(0, row)
        def _(k):
            i = row - 1 - k

            @pl.loop(0, i + 1)
            def _(j):
                raw_copy(i, j, row).wait_recv()
                pair_copy(i, j).start()

        @pl.loop(0, row)
        def _(j):
            coef[j] = -dot_n(di[...], sf[:, columns_of(j)])

        @pl.loop(0, row)
        def _(k):
            j = row - 1 - k
            high, low = split(coef[j])
            pair_copy(j, j).wait_recv()
            inverse = raw[j, j].astype(jnp.bfloat16)
            high, low = split(dot_n(high, inverse) + dot_n(low, inverse))
            g_high[j] = high
            g_low[j] = low

            @pl.loop(0, j)
            def _(i):
                pair_copy(j, i).wait_recv()
                factor = raw[j, i].astype(jnp.bfloat16)
                coef[i] = coef[i] - dot_n(g_high[j], factor) - dot_n(g_low[j], factor)

    def sol_copy(owner, h, to):
        source = part.at[p, half(h)] if gathered else out_ref.at[half(h)]
        return pltpu.make_async_remote_copy(
            src_ref=source, dst_ref=sol.at[owner, half(h)],
            send_sem=sol_send.at[to, h], recv_sem=sol_recv.at[owner, h],
            device_id={"row": to}, device_id_type=MESH,
        )

    def send_on(h):
        @pl.loop(row + 1, n_row)
        def _(j):
            sol_copy(row, h, j).start()

    def finish_sum(h):
        part[p, half(h)] = z_v[half(h)] - part[p, half(h)]

        @pl.when(p > 0)
        def _():
            line_move(line.at[0, p, half(h)], 0, p, h).wait_recv()
            part[p, half(h)] = part[p, half(h)] - line[0, p, half(h)]

        @pl.when(p < n_z - 1)
        def _():
            line_move(line.at[1, p, half(h)], 1, p, h).wait_recv()
            part[p, half(h)] = part[p, half(h)] - line[1, p, half(h)]

    def apply_rows(h):
        out_ref[half(h)] = dot_split(part[p, half(h)], di[...])

        @pl.loop(0, row)
        def _(j):
            sol_copy(j, h, row).wait_recv()
            high, low = split(sol[j, half(h)])
            out_ref[half(h)] = out_ref[half(h)] + (
                dot_t(high, g_high[j]) + dot_t(low, g_high[j]) + dot_t(high, g_low[j])
            )

    def chain_rows(h):
        @pl.loop(0, row)
        def _(j):
            sol_copy(j, h, row).wait_recv()
            part[p, half(h)] = part[p, half(h)] - dot_split(sol[j, half(h)], sf[:, columns_of(j)])

        out_ref[half(h)] = dot_split(part[p, half(h)], di[...])
        send_on(h)

    if gathered:
        for h in range(HALVES + 1):
            if h < HALVES:
                finish_sum(h)
                send_on(h)
            if h > 0:
                apply_rows(h - 1)

        @pl.loop(row + 1, n_row)
        def _(to):
            @pl.loop(0, row + 1)
            def _(j):
                raw_copy(row, j, to).wait_send()

        @pl.loop(0, row)
        def _(i):
            @pl.loop(0, i + 1)
            def _(j):
                pair_copy(i, j).wait_send()
    else:
        for h in range(HALVES):
            finish_sum(h)
            chain_rows(h)

    for h in range(HALVES):
        @pl.loop(row + 1, n_row)
        def _(j):
            sol_copy(row, h, j).wait_send()

    @pl.loop(0, n_z)
    def _(t):
        core_copy(t).wait_send()
        for h in range(HALVES):
            @pl.when((p < n_z - 1) & (t > p))
            def _():
                line_move(line.at[0, t, half(h)], 0, t, h).wait_send()

            @pl.when((p > 0) & (t < p))
            def _():
                line_move(line.at[1, t, half(h)], 1, t, h).wait_send()


def on_device(n_row, n_col, z_slab, prev_factor, prev_solution, slab_factor, diag_inverse):
    m, block = z_slab.shape
    n_z = n_col // CORES
    anywhere = pl.BlockSpec(memory_space=pltpu.HBM)
    f32 = jnp.float32
    held = n_row if n_row <= GATHER_ROWS else 1
    return pl.pallas_call(
        functools.partial(kernel, n_row, n_col),
        out_shape=jax.ShapeDtypeStruct((m, block), f32),
        in_specs=[anywhere] * 5,
        out_specs=pl.BlockSpec(memory_space=pltpu.VMEM),
        scratch_shapes=[
            pltpu.VMEM(z_slab.shape, f32),
            pltpu.VMEM(prev_factor.shape, prev_factor.dtype),
            pltpu.VMEM(prev_solution.shape, prev_solution.dtype),
            pltpu.VMEM(slab_factor.shape, slab_factor.dtype),
            pltpu.VMEM(diag_inverse.shape, diag_inverse.dtype),
            pltpu.VMEM((n_z, m, block), f32),
            pltpu.VMEM((n_z, m, block), f32),
            pltpu.VMEM((n_z, m, block), f32),
            pltpu.VMEM((2, n_z, m, block), f32),
            pltpu.VMEM((n_row, m, block), f32),
            pltpu.SemaphoreType.DMA((4,)),
            pltpu.SemaphoreType.DMA((n_z,)),
            pltpu.SemaphoreType.DMA((n_z,)),
            pltpu.SemaphoreType.DMA((n_z,)),
            pltpu.SemaphoreType.DMA((2, n_z, HALVES)),
            pltpu.SemaphoreType.DMA((2, n_z, HALVES)),
            pltpu.SemaphoreType.DMA((n_row, HALVES)),
            pltpu.SemaphoreType.DMA((n_row, HALVES)),
            pltpu.VMEM((held, held, block, block), f32),
            pltpu.VMEM((held, block, block), f32),
            pltpu.VMEM((held, block, block), jnp.bfloat16),
            pltpu.VMEM((held, block, block), jnp.bfloat16),
            pltpu.SemaphoreType.DMA((held, held)),
            pltpu.SemaphoreType.DMA((held, held)),
            pltpu.SemaphoreType.DMA((held, held)),
            pltpu.SemaphoreType.DMA((held, held)),
        ],
        compiler_params=pltpu.CompilerParams(
            collective_id=0, has_side_effects=True, vmem_limit_bytes=60 * 2**20
        ),
    )(z_slab, prev_factor, prev_solution, slab_factor, diag_inverse)


def solution(mesh):
    in_specs = (P("col", "row"), P("row", "col"), P(None, "col"), P("row", None), P("row", None))
    return jax.shard_map(
        functools.partial(on_device, mesh.shape["row"], mesh.shape["col"]),
        mesh=mesh, in_specs=in_specs, out_specs=P("col", "row"), check_vma=False,
    )
```

```python
import functools

import jax
import jax.numpy as jnp
from jax import lax
from jax.experimental import pallas as pl
from jax.experimental.pallas import tpu as pltpu
from jax.sharding import PartitionSpec as P

MESH = pl.DeviceIdType.MESH
CORES = 2
HALVES = 2
GATHER_ROWS = 4


def dot_t(left, right):
    return lax.dot_general(
        left, right, (((1,), (1,)), ((), ())), preferred_element_type=jnp.float32
    )


def dot_split(left, right):
    high = left.astype(jnp.bfloat16)
    low = (left - high.astype(jnp.float32)).astype(jnp.bfloat16)
    return dot_t(high, right) + dot_t(low, right)


def dot_n(left, right):
    return jnp.dot(left, right, preferred_element_type=jnp.float32)


def split(value):
    high = value.astype(jnp.bfloat16)
    return high, (value - high.astype(jnp.float32)).astype(jnp.bfloat16)


def kernel(
    n_row, n_col,
    z_hbm, pf_hbm, ps_hbm, sf_hbm, di_hbm,
    out_ref,
    z_v, pf, ps, sf, di, part, give, got, line, sol,
    load_sem, ps_sem, core_send, core_recv, line_send, line_recv, sol_send, sol_recv,
    pf_t, raw, coef, g_high, g_low, raw_send, raw_recv, pair_send, pair_recv,
):
    gathered = n_row <= GATHER_ROWS
    n_z = n_col // CORES
    m, block = z_v.shape
    mh = m // HALVES
    row = lax.axis_index("row")
    col = lax.axis_index("col")
    p = col // CORES
    core = lax.rem(col, CORES)
    mate = col + 1 - 2 * core
    chunk = CORES * m
    low_half = p < n_z // 2

    barrier = pltpu.get_barrier_semaphore()

    def greet(device):
        pl.semaphore_signal(barrier, inc=1, device_id=device, device_id_type=MESH)

    greet({"col": mate})

    @pl.when(p > 0)
    def _():
        greet({"col": col - CORES})

    @pl.when(p < n_z - 1)
    def _():
        greet({"col": col + CORES})

    for other in range(n_row):
        @pl.when(row != other)
        def _():
            greet({"row": other})

    def target(i):
        return jnp.where(low_half, n_z - 1 - i, i)

    def ps_copy(i):
        rows = pl.ds(pl.multiple_of(target(i) * chunk, chunk), chunk)
        return pltpu.make_async_copy(ps_hbm.at[rows], ps.at[rows], ps_sem.at[i])

    pf_copy = pltpu.make_async_copy(pf_hbm, pf, load_sem.at[0])
    z_copy = pltpu.make_async_copy(z_hbm, z_v, load_sem.at[1])
    sf_copy = pltpu.make_async_copy(sf_hbm, sf, load_sem.at[2])
    di_copy = pltpu.make_async_copy(di_hbm, di, load_sem.at[3])
    sf_copy.start()
    di_copy.start()
    pf_copy.start()
    for i in range(n_z):
        ps_copy(i).start()
    z_copy.start()

    b_half = block // 2
    own_half = pl.ds(pl.multiple_of(core * b_half, b_half), b_half)

    def raw_copy(i, j, to):
        return pltpu.make_async_remote_copy(
            src_ref=raw.at[i, j, own_half], dst_ref=raw.at[i, j, own_half],
            send_sem=raw_send.at[to, j], recv_sem=raw_recv.at[i, j],
            device_id={"row": to}, device_id_type=MESH,
        )

    def pair_copy(i, j):
        return pltpu.make_async_remote_copy(
            src_ref=raw.at[i, j, own_half], dst_ref=raw.at[i, j, own_half],
            send_sem=pair_send.at[i, j], recv_sem=pair_recv.at[i, j],
            device_id={"col": mate}, device_id_type=MESH,
        )

    def columns_of(j):
        return pl.ds(pl.multiple_of(j * block, block), block)

    sf_copy.wait()
    di_copy.wait()
    if gathered:
        @pl.when(row < n_row - 1)
        def _():
            raw[row, row, own_half] = di[own_half].astype(jnp.float32)

            @pl.loop(0, row)
            def _(j):
                raw[row, j, own_half] = sf[own_half, columns_of(j)].astype(jnp.float32)

    pf_copy.wait()
    pf_t[...] = pf[...].T

    def core_copy(t):
        return pltpu.make_async_remote_copy(
            src_ref=give.at[t], dst_ref=got.at[t],
            send_sem=core_send.at[t], recv_sem=core_recv.at[t],
            device_id={"col": mate}, device_id_type=MESH,
        )

    def multiply(i):
        t = target(i)
        ps_copy(i).wait()
        rows = pl.multiple_of(t * chunk, chunk)
        theirs = ps[pl.ds(pl.multiple_of(rows + (1 - core) * m, m), m), :]
        give[t] = dot_n(theirs, pf_t[...])
        if isinstance(i, int):
            pl.semaphore_wait(
                barrier,
                n_row + (p > 0).astype(jnp.int32) + (p < n_z - 1).astype(jnp.int32),
            )
        core_copy(t).start()
        mine = ps[pl.ds(pl.multiple_of(rows + core * m, m), m), :]
        part[t] = dot_n(mine, pf_t[...])

    def half(h):
        return pl.ds(h * mh, mh)

    def line_move(source, d, t, h):
        return pltpu.make_async_remote_copy(
            src_ref=source, dst_ref=line.at[d, t, half(h)],
            send_sem=line_send.at[d, t, h], recv_sem=line_recv.at[d, t, h],
            device_id={"col": col + CORES * (1 - 2 * d)}, device_id_type=MESH,
        )

    def pair_sum(i):
        t = target(i)
        core_copy(t).wait_recv()
        part[t] = part[t] + got[t]

        @pl.when((p == 0) & (t > 0))
        def _():
            for h in range(HALVES):
                line_move(part.at[t, half(h)], 0, t, h).start()

        @pl.when((p == n_z - 1) & (t < n_z - 1))
        def _():
            for h in range(HALVES):
                line_move(part.at[t, half(h)], 1, t, h).start()

    multiply(0)
    if gathered:
        @pl.loop(row + 1, n_row)
        def _(to):
            @pl.loop(0, row + 1)
            def _(j):
                raw_copy(row, j, to).start()

    @pl.loop(1, n_z)
    def _(i):
        multiply(i)
        pair_sum(i - 1)

    pair_sum(n_z - 1)

    first = jnp.where(low_half, 0, 1)
    inner = (p > 0) & (p < n_z - 1)

    @pl.loop(0, n_z - 1)
    def _(i):
        for e in range(2):
            d = first if e == 0 else 1 - first
            t = jnp.where(d == 0, n_z - 1 - i, i)

            @pl.when(inner & jnp.where(d == 0, t > p, t < p))
            def _():
                for h in range(HALVES):
                    line_move(line.at[d, t, half(h)], d, t, h).wait_recv()
                    line[d, t, half(h)] = line[d, t, half(h)] + part[t, half(h)]
                    line_move(line.at[d, t, half(h)], d, t, h).start()

    z_copy.wait()
    if gathered:
        @pl.loop(0, row)
        def _(k):
            i = row - 1 - k

            @pl.loop(0, i + 1)
            def _(j):
                raw_copy(i, j, row).wait_recv()
                pair_copy(i, j).start()

        def set_rows(j, value):
            rows = columns_of(j)
            high, low = split(value.T)
            g_high[rows] = high
            g_low[rows] = low

        set_rows(row, di[...].astype(jnp.float32))

        @pl.loop(row + 1, n_row)
        def _(j):
            g_high[columns_of(j)] = jnp.zeros((block, block), jnp.bfloat16)
            g_low[columns_of(j)] = jnp.zeros((block, block), jnp.bfloat16)
            sol[j] = jnp.zeros((m, block), jnp.float32)

        @pl.loop(0, row)
        def _(j):
            coef[j] = -dot_n(di[...], sf[:, columns_of(j)])

        @pl.loop(0, row)
        def _(k):
            j = row - 1 - k
            high, low = split(coef[j])
            pair_copy(j, j).wait_recv()
            inverse = raw[j, j].astype(jnp.bfloat16)
            composed = dot_n(high, inverse) + dot_n(low, inverse)
            set_rows(j, composed)
            high, low = split(composed)

            @pl.loop(0, j)
            def _(i):
                pair_copy(j, i).wait_recv()
                factor = raw[j, i].astype(jnp.bfloat16)
                coef[i] = coef[i] - dot_n(high, factor) - dot_n(low, factor)

    def sol_copy(owner, h, to):
        source = sol.at[row, half(h)] if gathered else out_ref.at[half(h)]
        return pltpu.make_async_remote_copy(
            src_ref=source, dst_ref=sol.at[owner, half(h)],
            send_sem=sol_send.at[to, h], recv_sem=sol_recv.at[owner, h],
            device_id={"row": to}, device_id_type=MESH,
        )

    def send_on(h):
        @pl.loop(row + 1, n_row)
        def _(j):
            sol_copy(row, h, j).start()

    def finish_sum(h):
        part[p, half(h)] = z_v[half(h)] - part[p, half(h)]

        @pl.when(p > 0)
        def _():
            line_move(line.at[0, p, half(h)], 0, p, h).wait_recv()
            part[p, half(h)] = part[p, half(h)] - line[0, p, half(h)]

        @pl.when(p < n_z - 1)
        def _():
            line_move(line.at[1, p, half(h)], 1, p, h).wait_recv()
            part[p, half(h)] = part[p, half(h)] - line[1, p, half(h)]

    def apply_rows(h):
        @pl.loop(0, row)
        def _(j):
            sol_copy(j, h, row).wait_recv()

        remainders = jnp.concatenate([sol[j, half(h)] for j in range(n_row)], axis=1)
        high, low = split(remainders)
        both = dot_n(jnp.concatenate([high, low], axis=0), g_high[...])
        out_ref[half(h)] = both[:mh] + both[mh:] + dot_n(high, g_low[...])

    def chain_rows(h):
        @pl.loop(0, row)
        def _(j):
            sol_copy(j, h, row).wait_recv()
            part[p, half(h)] = part[p, half(h)] - dot_split(sol[j, half(h)], sf[:, columns_of(j)])

        out_ref[half(h)] = dot_split(part[p, half(h)], di[...])
        send_on(h)

    if gathered:
        for h in range(HALVES + 1):
            if h < HALVES:
                finish_sum(h)
                sol[row, half(h)] = part[p, half(h)]
                send_on(h)
            if h > 0:
                apply_rows(h - 1)

        @pl.loop(row + 1, n_row)
        def _(to):
            @pl.loop(0, row + 1)
            def _(j):
                raw_copy(row, j, to).wait_send()

        @pl.loop(0, row)
        def _(i):
            @pl.loop(0, i + 1)
            def _(j):
                pair_copy(i, j).wait_send()
    else:
        for h in range(HALVES):
            finish_sum(h)
            chain_rows(h)

    for h in range(HALVES):
        @pl.loop(row + 1, n_row)
        def _(j):
            sol_copy(row, h, j).wait_send()

    @pl.loop(0, n_z)
    def _(t):
        core_copy(t).wait_send()
        for h in range(HALVES):
            @pl.when((p < n_z - 1) & (t > p))
            def _():
                line_move(line.at[0, t, half(h)], 0, t, h).wait_send()

            @pl.when((p > 0) & (t < p))
            def _():
                line_move(line.at[1, t, half(h)], 1, t, h).wait_send()


def on_device(n_row, n_col, z_slab, prev_factor, prev_solution, slab_factor, diag_inverse):
    m, block = z_slab.shape
    n_z = n_col // CORES
    anywhere = pl.BlockSpec(memory_space=pltpu.HBM)
    f32 = jnp.float32
    held = n_row if n_row <= GATHER_ROWS else 1
    return pl.pallas_call(
        functools.partial(kernel, n_row, n_col),
        out_shape=jax.ShapeDtypeStruct((m, block), f32),
        in_specs=[anywhere] * 5,
        out_specs=pl.BlockSpec(memory_space=pltpu.VMEM),
        scratch_shapes=[
            pltpu.VMEM(z_slab.shape, f32),
            pltpu.VMEM(prev_factor.shape, prev_factor.dtype),
            pltpu.VMEM(prev_solution.shape, prev_solution.dtype),
            pltpu.VMEM(slab_factor.shape, slab_factor.dtype),
            pltpu.VMEM(diag_inverse.shape, diag_inverse.dtype),
            pltpu.VMEM((n_z, m, block), f32),
            pltpu.VMEM((n_z, m, block), f32),
            pltpu.VMEM((n_z, m, block), f32),
            pltpu.VMEM((2, n_z, m, block), f32),
            pltpu.VMEM((n_row, m, block), f32),
            pltpu.SemaphoreType.DMA((4,)),
            pltpu.SemaphoreType.DMA((n_z,)),
            pltpu.SemaphoreType.DMA((n_z,)),
            pltpu.SemaphoreType.DMA((n_z,)),
            pltpu.SemaphoreType.DMA((2, n_z, HALVES)),
            pltpu.SemaphoreType.DMA((2, n_z, HALVES)),
            pltpu.SemaphoreType.DMA((n_row, HALVES)),
            pltpu.SemaphoreType.DMA((n_row, HALVES)),
            pltpu.VMEM(prev_factor.shape[::-1], prev_factor.dtype),
            pltpu.VMEM((held, held, block, block), f32),
            pltpu.VMEM((held, block, block), f32),
            pltpu.VMEM((held * block, block), jnp.bfloat16),
            pltpu.VMEM((held * block, block), jnp.bfloat16),
            pltpu.SemaphoreType.DMA((held, held)),
            pltpu.SemaphoreType.DMA((held, held)),
            pltpu.SemaphoreType.DMA((held, held)),
            pltpu.SemaphoreType.DMA((held, held)),
        ],
        compiler_params=pltpu.CompilerParams(
            collective_id=0, has_side_effects=True, vmem_limit_bytes=60 * 2**20
        ),
    )(z_slab, prev_factor, prev_solution, slab_factor, diag_inverse)


def solution(mesh):
    in_specs = (P("col", "row"), P("row", "col"), P(None, "col"), P("row", None), P("row", None))
    return jax.shard_map(
        functools.partial(on_device, mesh.shape["row"], mesh.shape["col"]),
        mesh=mesh, in_specs=in_specs, out_specs=P("col", "row"), check_vma=False,
    )
```

```python
import functools

import jax
import jax.numpy as jnp
from jax import lax
from jax.experimental import pallas as pl
from jax.experimental.pallas import tpu as pltpu
from jax.sharding import PartitionSpec as P

MESH = pl.DeviceIdType.MESH
CORES = 2
HALVES = 2
GATHER_ROWS = 4


def dot_t(left, right):
    return lax.dot_general(
        left, right, (((1,), (1,)), ((), ())), preferred_element_type=jnp.float32
    )


def dot_split(left, right):
    high = left.astype(jnp.bfloat16)
    low = (left - high.astype(jnp.float32)).astype(jnp.bfloat16)
    return dot_t(high, right) + dot_t(low, right)


def dot_n(left, right):
    return jnp.dot(left, right, preferred_element_type=jnp.float32)


def split(value):
    high = value.astype(jnp.bfloat16)
    return high, (value - high.astype(jnp.float32)).astype(jnp.bfloat16)


def kernel(
    n_row, n_col,
    z_hbm, pf_hbm, ps_hbm, sf_hbm, di_hbm,
    out_ref,
    z_v, pf, ps, sf, di, part, give, got, line, sol,
    load_sem, ps_sem, core_send, core_recv, line_send, line_recv, sol_send, sol_recv,
    pf_t, raw, coef, g_high, g_low, raw_send, raw_recv, pair_send, pair_recv,
):
    gathered = n_row <= GATHER_ROWS
    n_z = n_col // CORES
    m, block = z_v.shape
    mh = m // HALVES
    row = lax.axis_index("row")
    col = lax.axis_index("col")
    p = col // CORES
    core = lax.rem(col, CORES)
    mate = col + 1 - 2 * core
    chunk = CORES * m
    low_half = p < n_z // 2

    barrier = pltpu.get_barrier_semaphore()

    def greet(device):
        pl.semaphore_signal(barrier, inc=1, device_id=device, device_id_type=MESH)

    greet({"col": mate})

    @pl.when(p > 0)
    def _():
        greet({"col": col - CORES})

    @pl.when(p < n_z - 1)
    def _():
        greet({"col": col + CORES})

    for other in range(n_row):
        @pl.when(row != other)
        def _():
            greet({"row": other})

    def target(i):
        return jnp.where(low_half, n_z - 1 - i, i)

    def ps_copy(i):
        rows = pl.ds(pl.multiple_of(target(i) * chunk, chunk), chunk)
        return pltpu.make_async_copy(ps_hbm.at[rows], ps.at[rows], ps_sem.at[i])

    pf_copy = pltpu.make_async_copy(pf_hbm, pf, load_sem.at[0])
    z_copy = pltpu.make_async_copy(z_hbm, z_v, load_sem.at[1])
    sf_copy = pltpu.make_async_copy(sf_hbm, sf, load_sem.at[2])
    di_copy = pltpu.make_async_copy(di_hbm, di, load_sem.at[3])
    pf_copy.start()
    ps_copy(0).start()
    sf_copy.start()
    di_copy.start()
    for i in range(1, n_z):
        ps_copy(i).start()
    z_copy.start()

    b_half = block // 2
    own_half = pl.ds(pl.multiple_of(core * b_half, b_half), b_half)

    def raw_copy(i, j, to):
        return pltpu.make_async_remote_copy(
            src_ref=raw.at[i, j, own_half], dst_ref=raw.at[i, j, own_half],
            send_sem=raw_send.at[to, j], recv_sem=raw_recv.at[i, j],
            device_id={"row": to}, device_id_type=MESH,
        )

    def pair_copy(i, j):
        return pltpu.make_async_remote_copy(
            src_ref=raw.at[i, j, own_half], dst_ref=raw.at[i, j, own_half],
            send_sem=pair_send.at[i, j], recv_sem=pair_recv.at[i, j],
            device_id={"col": mate}, device_id_type=MESH,
        )

    def columns_of(j):
        return pl.ds(pl.multiple_of(j * block, block), block)

    pf_copy.wait()
    pf_t[...] = pf[...].T

    def core_copy(t):
        return pltpu.make_async_remote_copy(
            src_ref=give.at[t], dst_ref=got.at[t],
            send_sem=core_send.at[t], recv_sem=core_recv.at[t],
            device_id={"col": mate}, device_id_type=MESH,
        )

    def multiply(i):
        t = target(i)
        ps_copy(i).wait()
        rows = pl.multiple_of(t * chunk, chunk)
        theirs = ps[pl.ds(pl.multiple_of(rows + (1 - core) * m, m), m), :]
        give[t] = dot_n(theirs, pf_t[...])
        if isinstance(i, int):
            pl.semaphore_wait(
                barrier,
                n_row + (p > 0).astype(jnp.int32) + (p < n_z - 1).astype(jnp.int32),
            )
        core_copy(t).start()
        mine = ps[pl.ds(pl.multiple_of(rows + core * m, m), m), :]
        part[t] = dot_n(mine, pf_t[...])

    def half(h):
        return pl.ds(h * mh, mh)

    def line_move(source, d, t, h):
        return pltpu.make_async_remote_copy(
            src_ref=source, dst_ref=line.at[d, t, half(h)],
            send_sem=line_send.at[d, t, h], recv_sem=line_recv.at[d, t, h],
            device_id={"col": col + CORES * (1 - 2 * d)}, device_id_type=MESH,
        )

    def pair_sum(i):
        t = target(i)
        core_copy(t).wait_recv()
        part[t] = part[t] + got[t]

        @pl.when((p == 0) & (t > 0))
        def _():
            for h in range(HALVES):
                line_move(part.at[t, half(h)], 0, t, h).start()

        @pl.when((p == n_z - 1) & (t < n_z - 1))
        def _():
            for h in range(HALVES):
                line_move(part.at[t, half(h)], 1, t, h).start()

    multiply(0)
    sf_copy.wait()
    di_copy.wait()
    if gathered:
        @pl.when(row < n_row - 1)
        def _():
            raw[row, row, own_half] = di[own_half].astype(jnp.float32)

            @pl.loop(0, row)
            def _(j):
                raw[row, j, own_half] = sf[own_half, columns_of(j)].astype(jnp.float32)

    if gathered:
        @pl.loop(row + 1, n_row)
        def _(to):
            @pl.loop(0, row + 1)
            def _(j):
                raw_copy(row, j, to).start()

    pair_sum(0)

    @pl.loop(1, n_z)
    def _(i):
        multiply(i)
        pair_sum(i)

    first = jnp.where(low_half, 0, 1)
    inner = (p > 0) & (p < n_z - 1)

    @pl.loop(0, n_z - 1)
    def _(i):
        for e in range(2):
            d = first if e == 0 else 1 - first
            t = jnp.where(d == 0, n_z - 1 - i, i)

            @pl.when(inner & jnp.where(d == 0, t > p, t < p))
            def _():
                for h in range(HALVES):
                    line_move(line.at[d, t, half(h)], d, t, h).wait_recv()
                    line[d, t, half(h)] = line[d, t, half(h)] + part[t, half(h)]
                    line_move(line.at[d, t, half(h)], d, t, h).start()

    z_copy.wait()
    if gathered:
        @pl.loop(0, row)
        def _(k):
            i = row - 1 - k

            @pl.loop(0, i + 1)
            def _(j):
                raw_copy(i, j, row).wait_recv()
                pair_copy(i, j).start()

        def set_rows(j, value):
            rows = columns_of(j)
            high, low = split(value.T)
            g_high[rows] = high
            g_low[rows] = low

        set_rows(row, di[...].astype(jnp.float32))

        @pl.loop(row + 1, n_row)
        def _(j):
            g_high[columns_of(j)] = jnp.zeros((block, block), jnp.bfloat16)
            g_low[columns_of(j)] = jnp.zeros((block, block), jnp.bfloat16)
            sol[j] = jnp.zeros((m, block), jnp.float32)

        @pl.loop(0, row)
        def _(j):
            coef[j] = -dot_n(di[...], sf[:, columns_of(j)])

        @pl.loop(0, row)
        def _(k):
            j = row - 1 - k
            high, low = split(coef[j])
            pair_copy(j, j).wait_recv()
            inverse = raw[j, j].astype(jnp.bfloat16)
            composed = dot_n(high, inverse) + dot_n(low, inverse)
            set_rows(j, composed)
            high, low = split(composed)

            @pl.loop(0, j)
            def _(i):
                pair_copy(j, i).wait_recv()
                factor = raw[j, i].astype(jnp.bfloat16)
                coef[i] = coef[i] - dot_n(high, factor) - dot_n(low, factor)

    def sol_copy(owner, h, to):
        source = sol.at[row, half(h)] if gathered else out_ref.at[half(h)]
        return pltpu.make_async_remote_copy(
            src_ref=source, dst_ref=sol.at[owner, half(h)],
            send_sem=sol_send.at[to, h], recv_sem=sol_recv.at[owner, h],
            device_id={"row": to}, device_id_type=MESH,
        )

    def send_on(h):
        @pl.loop(row + 1, n_row)
        def _(j):
            sol_copy(row, h, j).start()

    def finish_sum(h):
        part[p, half(h)] = z_v[half(h)] - part[p, half(h)]

        @pl.when(p > 0)
        def _():
            line_move(line.at[0, p, half(h)], 0, p, h).wait_recv()
            part[p, half(h)] = part[p, half(h)] - line[0, p, half(h)]

        @pl.when(p < n_z - 1)
        def _():
            line_move(line.at[1, p, half(h)], 1, p, h).wait_recv()
            part[p, half(h)] = part[p, half(h)] - line[1, p, half(h)]

    def apply_rows(h):
        @pl.loop(0, row)
        def _(j):
            sol_copy(j, h, row).wait_recv()

        remainders = jnp.concatenate([sol[j, half(h)] for j in range(n_row)], axis=1)
        high, low = split(remainders)
        both = dot_n(jnp.concatenate([high, low], axis=0), g_high[...])
        out_ref[half(h)] = both[:mh] + both[mh:] + dot_n(high, g_low[...])

    def chain_rows(h):
        @pl.loop(0, row)
        def _(j):
            sol_copy(j, h, row).wait_recv()
            part[p, half(h)] = part[p, half(h)] - dot_split(sol[j, half(h)], sf[:, columns_of(j)])

        out_ref[half(h)] = dot_split(part[p, half(h)], di[...])
        send_on(h)

    if gathered:
        for h in range(HALVES + 1):
            if h < HALVES:
                finish_sum(h)
                sol[row, half(h)] = part[p, half(h)]
                send_on(h)
            if h > 0:
                apply_rows(h - 1)

        @pl.loop(row + 1, n_row)
        def _(to):
            @pl.loop(0, row + 1)
            def _(j):
                raw_copy(row, j, to).wait_send()

        @pl.loop(0, row)
        def _(i):
            @pl.loop(0, i + 1)
            def _(j):
                pair_copy(i, j).wait_send()
    else:
        for h in range(HALVES):
            finish_sum(h)
            chain_rows(h)

    for h in range(HALVES):
        @pl.loop(row + 1, n_row)
        def _(j):
            sol_copy(row, h, j).wait_send()

    @pl.loop(0, n_z)
    def _(t):
        core_copy(t).wait_send()
        for h in range(HALVES):
            @pl.when((p < n_z - 1) & (t > p))
            def _():
                line_move(line.at[0, t, half(h)], 0, t, h).wait_send()

            @pl.when((p > 0) & (t < p))
            def _():
                line_move(line.at[1, t, half(h)], 1, t, h).wait_send()


def on_device(n_row, n_col, z_slab, prev_factor, prev_solution, slab_factor, diag_inverse):
    m, block = z_slab.shape
    n_z = n_col // CORES
    anywhere = pl.BlockSpec(memory_space=pltpu.HBM)
    f32 = jnp.float32
    held = n_row if n_row <= GATHER_ROWS else 1
    return pl.pallas_call(
        functools.partial(kernel, n_row, n_col),
        out_shape=jax.ShapeDtypeStruct((m, block), f32),
        in_specs=[anywhere] * 5,
        out_specs=pl.BlockSpec(memory_space=pltpu.VMEM),
        scratch_shapes=[
            pltpu.VMEM(z_slab.shape, f32),
            pltpu.VMEM(prev_factor.shape, prev_factor.dtype),
            pltpu.VMEM(prev_solution.shape, prev_solution.dtype),
            pltpu.VMEM(slab_factor.shape, slab_factor.dtype),
            pltpu.VMEM(diag_inverse.shape, diag_inverse.dtype),
            pltpu.VMEM((n_z, m, block), f32),
            pltpu.VMEM((n_z, m, block), f32),
            pltpu.VMEM((n_z, m, block), f32),
            pltpu.VMEM((2, n_z, m, block), f32),
            pltpu.VMEM((n_row, m, block), f32),
            pltpu.SemaphoreType.DMA((4,)),
            pltpu.SemaphoreType.DMA((n_z,)),
            pltpu.SemaphoreType.DMA((n_z,)),
            pltpu.SemaphoreType.DMA((n_z,)),
            pltpu.SemaphoreType.DMA((2, n_z, HALVES)),
            pltpu.SemaphoreType.DMA((2, n_z, HALVES)),
            pltpu.SemaphoreType.DMA((n_row, HALVES)),
            pltpu.SemaphoreType.DMA((n_row, HALVES)),
            pltpu.VMEM(prev_factor.shape[::-1], prev_factor.dtype),
            pltpu.VMEM((held, held, block, block), f32),
            pltpu.VMEM((held, block, block), f32),
            pltpu.VMEM((held * block, block), jnp.bfloat16),
            pltpu.VMEM((held * block, block), jnp.bfloat16),
            pltpu.SemaphoreType.DMA((held, held)),
            pltpu.SemaphoreType.DMA((held, held)),
            pltpu.SemaphoreType.DMA((held, held)),
            pltpu.SemaphoreType.DMA((held, held)),
        ],
        compiler_params=pltpu.CompilerParams(
            collective_id=0, has_side_effects=True, vmem_limit_bytes=60 * 2**20
        ),
    )(z_slab, prev_factor, prev_solution, slab_factor, diag_inverse)


def solution(mesh):
    in_specs = (P("col", "row"), P("row", "col"), P(None, "col"), P("row", None), P("row", None))
    return jax.shard_map(
        functools.partial(on_device, mesh.shape["row"], mesh.shape["col"]),
        mesh=mesh, in_specs=in_specs, out_specs=P("col", "row"), check_vma=False,
    )
```

```python
import functools

import jax
import jax.numpy as jnp
from jax import lax
from jax.experimental import pallas as pl
from jax.experimental.pallas import tpu as pltpu
from jax.sharding import PartitionSpec as P

MESH = pl.DeviceIdType.MESH
CORES = 2
HALVES = 2
GATHER_ROWS = 4


def dot_t(left, right):
    return lax.dot_general(
        left, right, (((1,), (1,)), ((), ())), preferred_element_type=jnp.float32
    )


def dot_split(left, right):
    high = left.astype(jnp.bfloat16)
    low = (left - high.astype(jnp.float32)).astype(jnp.bfloat16)
    return dot_t(high, right) + dot_t(low, right)


def dot_n(left, right):
    return jnp.dot(left, right, preferred_element_type=jnp.float32)


def split(value):
    high = value.astype(jnp.bfloat16)
    return high, (value - high.astype(jnp.float32)).astype(jnp.bfloat16)


def kernel(
    n_row, n_col,
    z_hbm, pf_hbm, ps_hbm, sf_hbm, di_hbm,
    out_ref,
    z_v, pf, ps, sf, di, part, give, got, line, sol,
    load_sem, ps_sem, core_send, core_recv, line_send, line_recv, sol_send, sol_recv,
    pf_t, raw, coef, g_high, g_low, raw_send, raw_recv, pair_send, pair_recv,
):
    gathered = n_row <= GATHER_ROWS
    n_z = n_col // CORES
    m, block = z_v.shape
    mh = m // HALVES
    row = lax.axis_index("row")
    col = lax.axis_index("col")
    p = col // CORES
    core = lax.rem(col, CORES)
    mate = col + 1 - 2 * core
    chunk = CORES * m
    low_half = p < n_z // 2

    barrier = pltpu.get_barrier_semaphore()

    def greet(device):
        pl.semaphore_signal(barrier, inc=1, device_id=device, device_id_type=MESH)

    greet({"col": mate})

    @pl.when(p > 0)
    def _():
        greet({"col": col - CORES})

    @pl.when(p < n_z - 1)
    def _():
        greet({"col": col + CORES})

    for other in range(n_row):
        @pl.when(row != other)
        def _():
            greet({"row": other})

    def target(i):
        return jnp.where(low_half, n_z - 1 - i, i)

    def ps_copy(i):
        rows = pl.ds(pl.multiple_of(target(i) * chunk, chunk), chunk)
        return pltpu.make_async_copy(ps_hbm.at[rows], ps.at[rows], ps_sem.at[i])

    pf_copy = pltpu.make_async_copy(pf_hbm, pf, load_sem.at[0])
    z_copy = pltpu.make_async_copy(z_hbm, z_v, load_sem.at[1])
    sf_copy = pltpu.make_async_copy(sf_hbm, sf, load_sem.at[2])
    di_copy = pltpu.make_async_copy(di_hbm, di, load_sem.at[3])
    pf_copy.start()
    ps_copy(0).start()
    sf_copy.start()
    di_copy.start()
    for i in range(1, n_z):
        ps_copy(i).start()
    z_copy.start()

    b_half = block // 2
    own_half = pl.ds(pl.multiple_of(core * b_half, b_half), b_half)

    def raw_copy(i, j, to):
        return pltpu.make_async_remote_copy(
            src_ref=raw.at[i, j, own_half], dst_ref=raw.at[i, j, own_half],
            send_sem=raw_send.at[to, j], recv_sem=raw_recv.at[i, j],
            device_id={"row": to}, device_id_type=MESH,
        )

    def pair_copy(i, j):
        return pltpu.make_async_remote_copy(
            src_ref=raw.at[i, j, own_half], dst_ref=raw.at[i, j, own_half],
            send_sem=pair_send.at[i, j], recv_sem=pair_recv.at[i, j],
            device_id={"col": mate}, device_id_type=MESH,
        )

    def columns_of(j):
        return pl.ds(pl.multiple_of(j * block, block), block)

    pf_copy.wait()
    pf_t[...] = pf[...].T

    def core_copy(t, h):
        return pltpu.make_async_remote_copy(
            src_ref=give.at[t, half(h)], dst_ref=got.at[t, half(h)],
            send_sem=core_send.at[t, h], recv_sem=core_recv.at[t, h],
            device_id={"col": mate}, device_id_type=MESH,
        )

    def multiply(i):
        t = target(i)
        ps_copy(i).wait()
        rows = pl.multiple_of(t * chunk, chunk)
        theirs = ps[pl.ds(pl.multiple_of(rows + (1 - core) * m, m), m), :]
        give[t] = dot_n(theirs, pf_t[...])
        if isinstance(i, int):
            pl.semaphore_wait(
                barrier,
                n_row + (p > 0).astype(jnp.int32) + (p < n_z - 1).astype(jnp.int32),
            )
        for h in range(HALVES):
            core_copy(t, h).start()
        mine = ps[pl.ds(pl.multiple_of(rows + core * m, m), m), :]
        part[t] = dot_n(mine, pf_t[...])

    def half(h):
        return pl.ds(h * mh, mh)

    def line_move(source, d, t, h):
        return pltpu.make_async_remote_copy(
            src_ref=source, dst_ref=line.at[d, t, half(h)],
            send_sem=line_send.at[d, t, h], recv_sem=line_recv.at[d, t, h],
            device_id={"col": col + CORES * (1 - 2 * d)}, device_id_type=MESH,
        )

    def pair_sum(i):
        t = target(i)
        for h in range(HALVES):
            core_copy(t, h).wait_recv()
            part[t, half(h)] = part[t, half(h)] + got[t, half(h)]

            @pl.when((p == 0) & (t > 0))
            def _():
                line_move(part.at[t, half(h)], 0, t, h).start()

            @pl.when((p == n_z - 1) & (t < n_z - 1))
            def _():
                line_move(part.at[t, half(h)], 1, t, h).start()

    multiply(0)
    sf_copy.wait()
    di_copy.wait()
    if gathered:
        @pl.when(row < n_row - 1)
        def _():
            raw[row, row, own_half] = di[own_half].astype(jnp.float32)

            @pl.loop(0, row)
            def _(j):
                raw[row, j, own_half] = sf[own_half, columns_of(j)].astype(jnp.float32)

    if gathered:
        @pl.loop(row + 1, n_row)
        def _(to):
            @pl.loop(0, row + 1)
            def _(j):
                raw_copy(row, j, to).start()

    pair_sum(0)

    @pl.loop(1, n_z)
    def _(i):
        multiply(i)
        pair_sum(i)

    first = jnp.where(low_half, 0, 1)
    inner = (p > 0) & (p < n_z - 1)

    @pl.loop(0, n_z - 1)
    def _(i):
        for e in range(2):
            d = first if e == 0 else 1 - first
            t = jnp.where(d == 0, n_z - 1 - i, i)

            @pl.when(inner & jnp.where(d == 0, t > p, t < p))
            def _():
                for h in range(HALVES):
                    line_move(line.at[d, t, half(h)], d, t, h).wait_recv()
                    line[d, t, half(h)] = line[d, t, half(h)] + part[t, half(h)]
                    line_move(line.at[d, t, half(h)], d, t, h).start()

    z_copy.wait()
    if gathered:
        @pl.loop(0, row)
        def _(k):
            i = row - 1 - k

            @pl.loop(0, i + 1)
            def _(j):
                raw_copy(i, j, row).wait_recv()
                pair_copy(i, j).start()

        def set_rows(j, value):
            rows = columns_of(j)
            high, low = split(value.T)
            g_high[rows] = high
            g_low[rows] = low

        set_rows(row, di[...].astype(jnp.float32))

        @pl.loop(row + 1, n_row)
        def _(j):
            g_high[columns_of(j)] = jnp.zeros((block, block), jnp.bfloat16)
            g_low[columns_of(j)] = jnp.zeros((block, block), jnp.bfloat16)
            sol[j] = jnp.zeros((m, block), jnp.float32)

        @pl.loop(0, row)
        def _(j):
            coef[j] = -dot_n(di[...], sf[:, columns_of(j)])

        @pl.loop(0, row)
        def _(k):
            j = row - 1 - k
            high, low = split(coef[j])
            pair_copy(j, j).wait_recv()
            inverse = raw[j, j].astype(jnp.bfloat16)
            composed = dot_n(high, inverse) + dot_n(low, inverse)
            set_rows(j, composed)
            high, low = split(composed)

            @pl.loop(0, j)
            def _(i):
                pair_copy(j, i).wait_recv()
                factor = raw[j, i].astype(jnp.bfloat16)
                coef[i] = coef[i] - dot_n(high, factor) - dot_n(low, factor)

    def sol_copy(owner, h, to):
        source = sol.at[row, half(h)] if gathered else out_ref.at[half(h)]
        return pltpu.make_async_remote_copy(
            src_ref=source, dst_ref=sol.at[owner, half(h)],
            send_sem=sol_send.at[to, h], recv_sem=sol_recv.at[owner, h],
            device_id={"row": to}, device_id_type=MESH,
        )

    def send_on(h):
        @pl.loop(row + 1, n_row)
        def _(j):
            sol_copy(row, h, j).start()

    def finish_sum(h):
        part[p, half(h)] = z_v[half(h)] - part[p, half(h)]

        @pl.when(p > 0)
        def _():
            line_move(line.at[0, p, half(h)], 0, p, h).wait_recv()
            part[p, half(h)] = part[p, half(h)] - line[0, p, half(h)]

        @pl.when(p < n_z - 1)
        def _():
            line_move(line.at[1, p, half(h)], 1, p, h).wait_recv()
            part[p, half(h)] = part[p, half(h)] - line[1, p, half(h)]

    def apply_rows(h):
        @pl.loop(0, row)
        def _(j):
            sol_copy(j, h, row).wait_recv()

        remainders = jnp.concatenate([sol[j, half(h)] for j in range(n_row)], axis=1)
        high, low = split(remainders)
        both = dot_n(jnp.concatenate([high, low], axis=0), g_high[...])
        out_ref[half(h)] = both[:mh] + both[mh:] + dot_n(high, g_low[...])

    def chain_rows(h):
        @pl.loop(0, row)
        def _(j):
            sol_copy(j, h, row).wait_recv()
            part[p, half(h)] = part[p, half(h)] - dot_split(sol[j, half(h)], sf[:, columns_of(j)])

        out_ref[half(h)] = dot_split(part[p, half(h)], di[...])
        send_on(h)

    if gathered:
        for h in range(HALVES + 1):
            if h < HALVES:
                finish_sum(h)
                sol[row, half(h)] = part[p, half(h)]
                send_on(h)
            if h > 0:
                apply_rows(h - 1)

        @pl.loop(row + 1, n_row)
        def _(to):
            @pl.loop(0, row + 1)
            def _(j):
                raw_copy(row, j, to).wait_send()

        @pl.loop(0, row)
        def _(i):
            @pl.loop(0, i + 1)
            def _(j):
                pair_copy(i, j).wait_send()
    else:
        for h in range(HALVES):
            finish_sum(h)
            chain_rows(h)

    for h in range(HALVES):
        @pl.loop(row + 1, n_row)
        def _(j):
            sol_copy(row, h, j).wait_send()

    @pl.loop(0, n_z)
    def _(t):
        for h in range(HALVES):
            core_copy(t, h).wait_send()

            @pl.when((p < n_z - 1) & (t > p))
            def _():
                line_move(line.at[0, t, half(h)], 0, t, h).wait_send()

            @pl.when((p > 0) & (t < p))
            def _():
                line_move(line.at[1, t, half(h)], 1, t, h).wait_send()


def on_device(n_row, n_col, z_slab, prev_factor, prev_solution, slab_factor, diag_inverse):
    m, block = z_slab.shape
    n_z = n_col // CORES
    anywhere = pl.BlockSpec(memory_space=pltpu.HBM)
    f32 = jnp.float32
    held = n_row if n_row <= GATHER_ROWS else 1
    return pl.pallas_call(
        functools.partial(kernel, n_row, n_col),
        out_shape=jax.ShapeDtypeStruct((m, block), f32),
        in_specs=[anywhere] * 5,
        out_specs=pl.BlockSpec(memory_space=pltpu.VMEM),
        scratch_shapes=[
            pltpu.VMEM(z_slab.shape, f32),
            pltpu.VMEM(prev_factor.shape, prev_factor.dtype),
            pltpu.VMEM(prev_solution.shape, prev_solution.dtype),
            pltpu.VMEM(slab_factor.shape, slab_factor.dtype),
            pltpu.VMEM(diag_inverse.shape, diag_inverse.dtype),
            pltpu.VMEM((n_z, m, block), f32),
            pltpu.VMEM((n_z, m, block), f32),
            pltpu.VMEM((n_z, m, block), f32),
            pltpu.VMEM((2, n_z, m, block), f32),
            pltpu.VMEM((n_row, m, block), f32),
            pltpu.SemaphoreType.DMA((4,)),
            pltpu.SemaphoreType.DMA((n_z,)),
            pltpu.SemaphoreType.DMA((n_z, HALVES)),
            pltpu.SemaphoreType.DMA((n_z, HALVES)),
            pltpu.SemaphoreType.DMA((2, n_z, HALVES)),
            pltpu.SemaphoreType.DMA((2, n_z, HALVES)),
            pltpu.SemaphoreType.DMA((n_row, HALVES)),
            pltpu.SemaphoreType.DMA((n_row, HALVES)),
            pltpu.VMEM(prev_factor.shape[::-1], prev_factor.dtype),
            pltpu.VMEM((held, held, block, block), f32),
            pltpu.VMEM((held, block, block), f32),
            pltpu.VMEM((held * block, block), jnp.bfloat16),
            pltpu.VMEM((held * block, block), jnp.bfloat16),
            pltpu.SemaphoreType.DMA((held, held)),
            pltpu.SemaphoreType.DMA((held, held)),
            pltpu.SemaphoreType.DMA((held, held)),
            pltpu.SemaphoreType.DMA((held, held)),
        ],
        compiler_params=pltpu.CompilerParams(
            collective_id=0, has_side_effects=True, vmem_limit_bytes=60 * 2**20
        ),
    )(z_slab, prev_factor, prev_solution, slab_factor, diag_inverse)


def solution(mesh):
    in_specs = (P("col", "row"), P("row", "col"), P(None, "col"), P("row", None), P("row", None))
    return jax.shard_map(
        functools.partial(on_device, mesh.shape["row"], mesh.shape["col"]),
        mesh=mesh, in_specs=in_specs, out_specs=P("col", "row"), check_vma=False,
    )
```
